512 devices in a mesh: leaf: 128 (over x, z, core), sub: 4 (over y).
Axes of the slice: x: 4, y: 4, z: 16, core: 2. Of those that a mesh axis runs over, the one named last changes fastest.
Arguments:
- probe_rhs: float32 [32, 524288], P(None, ('leaf', 'sub')), may hold values from -22.5 to 22.5
- coords: float32 [3, 524288], P(None, ('leaf', 'sub')), may hold values from -820.7 to 820.7
- near_list: int32 [2048, 5], P(('leaf', 'sub')), may hold values from -1 to 2047, as said below
- far_leaf_list: int32 [2048, 8], P(('leaf', 'sub')), may hold values from -1 to 2047, as said below
- far_group_list: int32 [128, 16], P('leaf'), may hold values from -1 to 127, as said below
- leaf_basis: float32 [2048, 64, 256], P(('leaf', 'sub')), may hold values from -0.375 to 0.375
- leaf_skeleton: float32 [3, 131072], P(None, ('leaf', 'sub')), may hold values from -820.7 to 820.7
- leaf_transfer: float32 [2048, 64, 64], P(('leaf', 'sub')), may hold values from -0.375 to 0.375
- device_transfer: float32 [512, 64, 64], P(('leaf', 'sub')), may hold values from -0.375 to 0.375
- group_skeleton: float32 [3, 8192], P(None, 'leaf'), may hold values from -1.5 to 4.5
Outputs:
- solution: float32 [32, 524288], P(None, ('leaf', 'sub'))
- residual: float32 [32, 524288], P(None, ('leaf', 'sub'))
The draws below stay inside these ranges and needn't reach their ends.
Inputs may be any that keep to these rules, and one draw needn't show every extreme that they name: `near_list`: row i names distinct leaves within 2 of i, always i itself, -1 in unused slots, in any order; j is named in row i exactly when i is named in row j. `far_leaf_list`: row i names distinct leaves of the same group of 16 consecutive leaves, each more than 2 away from i, -1 in unused slots, in any order; the relation is symmetric. `far_group_list`: row g names distinct groups other than g, -1 in unused slots, in any order; the relation is symmetric.
All inputs are finite; a program needn't handle non-finite values.
Results may differ from the reference program's by a relative error of at most 0.0003.
Values sent between devices are 32-bit elements; how exact they have to be, the bound alone decides.
A program may use at most 64 MiB of HBM per device.

```python
from functools import partial
import jax
import jax.numpy as jnp
from jax import lax

LEAF = 256
RANK = 64
PROBES = 32
REACH = 2
FAR_LEAF = 8
ITERS = 2
LEAVES_DEV = 4
GROUP_LEAVES = 16
NLEAF = 2048
NPTS = 524288
NGROUP = 128
FAR_GROUP = 16
N_SUB = 4
DEVICES = 512


def leaf_centers(key):
    steps_drawn = jax.random.uniform(jax.random.fold_in(key, 11), (3, NLEAF), jnp.float32, -0.4, 0.4)
    return jnp.cumsum(steps_drawn, axis=1)


def jitter_points(key, salt, count):
    return jnp.clip(0.5 * jax.random.normal(jax.random.fold_in(key, salt), (3, NLEAF, count), jnp.float32), -1.5, 1.5)


def draw_coords(key, part):
    centers = leaf_centers(key)
    return (centers[:, :, None] + jitter_points(key, 21, LEAF)).reshape(3, NPTS)


def draw_leaf_skeleton(key, part):
    centers = leaf_centers(key)
    return (centers[:, :, None] + jitter_points(key, 22, RANK)).reshape(3, NLEAF * RANK)


def draw_group_skeleton(key, part):
    centers = jax.random.uniform(jax.random.fold_in(key, 23), (3, NGROUP, 1), jnp.float32, 0.0, 3.0)
    jitter = jnp.clip(0.5 * jax.random.normal(jax.random.fold_in(key, 24), (3, NGROUP, RANK), jnp.float32), -1.5, 1.5)
    return (centers + jitter).reshape(3, NGROUP * RANK)


def draw_probe_rhs(key, part):
    rising = jnp.exp(jnp.log(3.0) * jnp.arange(NLEAF, dtype=jnp.float32) / NLEAF)
    rough = jax.random.uniform(jax.random.fold_in(key, 31), (NLEAF,), jnp.float32, 0.5, 1.5)
    scales = (rising * rough)[None, :, None]
    values = jnp.clip(jax.random.normal(jax.random.fold_in(key, 32), (PROBES, NLEAF, LEAF), jnp.float32), -5.0, 5.0)
    return (scales * values).reshape(PROBES, NPTS)


def pair_table(key, count, block, offsets, salt):
    positions = jnp.arange(count, dtype=jnp.int32)
    in_block = positions % block
    columns = []
    for column_index in range(offsets.shape[0]):
        offset = offsets[column_index]
        kept_pair = jax.random.randint(jax.random.fold_in(key, salt + column_index), (count,), 0, 4) > 0
        upper = jnp.where(kept_pair & (in_block + offset < block), positions + offset, -1)
        earlier = jnp.roll(kept_pair, offset)
        lower = jnp.where(earlier & (in_block - offset >= 0), positions - offset, -1)
        columns = columns + [upper, lower]
    return jnp.stack(columns, axis=1).astype(jnp.int32)


def draw_near_list(key, part):
    offsets = jnp.arange(1, REACH + 1, dtype=jnp.int32)
    table = pair_table(key, NLEAF, NLEAF, offsets, 100)
    itself = jnp.arange(NLEAF, dtype=jnp.int32)[:, None]
    table = jnp.concatenate([itself, table], axis=1)
    return jax.random.permutation(jax.random.fold_in(key, 101), table, axis=1, independent=True)


def draw_far_leaf_list(key, part):
    offsets = (jax.random.permutation(jax.random.fold_in(key, 200), GROUP_LEAVES - REACH - 1)[:FAR_LEAF // 2] + REACH + 1).astype(jnp.int32)
    table = pair_table(key, NLEAF, GROUP_LEAVES, offsets, 300)
    return jax.random.permutation(jax.random.fold_in(key, 301), table, axis=1, independent=True)


def draw_far_group_list(key, part):
    shuffled = (jax.random.permutation(jax.random.fold_in(key, 400), NGROUP - 1) + 1).astype(jnp.int32)
    places = jnp.arange(NGROUP - 1, dtype=jnp.int32)
    priority = jnp.where(shuffled == 1, -2, jnp.where(shuffled == NGROUP // 2, -1, places)).astype(jnp.int32)
    ordering = jnp.argsort(priority, stable=True)
    offsets = shuffled[ordering][:FAR_GROUP // 2].astype(jnp.int32)
    table = pair_table(key, NGROUP, NGROUP, offsets, 500)
    return jax.random.permutation(jax.random.fold_in(key, 501), table, axis=1, independent=True)


def block_scale(key, dims, split, least, high):
    def one(axis_at, parts):
        heights = jax.random.uniform(jax.random.fold_in(jax.random.fold_in(key, 6), axis_at), (parts,), jnp.float32, least / len(split), high / len(split))
        return jnp.repeat(jnp.exp(heights), dims[axis_at] // parts).reshape((-1,) + (1,) * (len(dims) - axis_at - 1))

    level = one(*split[0])
    for cut in split[1:]:
        level = level * one(*cut)
    return level


def centred(own_key, shape, deviation, most, shards=(), kind=jnp.bfloat16):
    entries = deviation * jax.random.normal(own_key, shape, jnp.float32)
    if shards:
        entries = entries * block_scale(own_key, shape, shards, -0.22, 0.18)
    return jnp.clip(entries, -most, most).astype(kind)


def setup_inputs(seed: int = 0) -> dict:
    splits = jax.random.split(jax.random.key(seed), 11)
    probe_rhs = draw_probe_rhs(jax.random.fold_in(splits[10], 71), 0)
    coords = draw_coords(jax.random.fold_in(splits[10], 71), 0)
    near_list = draw_near_list(jax.random.fold_in(splits[10], 71), 0)
    far_leaf_list = draw_far_leaf_list(jax.random.fold_in(splits[10], 71), 0)
    far_group_list = draw_far_group_list(jax.random.fold_in(splits[10], 71), 0)
    leaf_basis = centred(splits[5], (NLEAF, RANK, LEAF), LEAF ** -0.5, 0.375, ((0, 512),), jnp.float32)
    leaf_skeleton = draw_leaf_skeleton(jax.random.fold_in(splits[10], 71), 0)
    leaf_transfer = centred(splits[7], (NLEAF, RANK, RANK), (RANK * LEAVES_DEV) ** -0.5, 0.375, ((0, 512),), jnp.float32)
    device_transfer = centred(splits[8], (DEVICES, RANK, RANK), (RANK * N_SUB) ** -0.5, 0.375, ((0, 512),), jnp.float32)
    group_skeleton = draw_group_skeleton(jax.random.fold_in(splits[10], 71), 0)
    return dict(probe_rhs=probe_rhs, coords=coords, near_list=near_list, far_leaf_list=far_leaf_list, far_group_list=far_group_list, leaf_basis=leaf_basis, leaf_skeleton=leaf_skeleton, leaf_transfer=leaf_transfer, device_transfer=device_transfer, group_skeleton=group_skeleton)


NOISE = 1.0
ROOT_FIVE = 5.0 ** 0.5
HIGHEST = lax.Precision.HIGHEST

def matern(left_points, right_points):
    spread = left_points[..., :, :, None] - right_points[..., :, None, :]
    scaled = ROOT_FIVE * jnp.sqrt(lax.optimization_barrier(jnp.sum(spread * spread, axis=-3)))
    return (1.0 + scaled + scaled * scaled / 3.0) * jnp.exp(-scaled)

def apply_operator(vectors, coords, near_list, far_leaf_list, far_group_list, leaf_basis, leaf_skeleton, leaf_transfer, device_transfer, group_skeleton):
    leaves = near_list.shape[0]
    groups = far_group_list.shape[0]
    devices = device_transfer.shape[0]
    by_leaf = vectors.reshape(PROBES, leaves, LEAF)
    points = coords.reshape(3, leaves, LEAF)

    def near_leaf(leaf_index):
        own_points = points[:, leaf_index]
        totals = jnp.zeros((PROBES, LEAF), jnp.float32)
        for column in range(near_list.shape[1]):
            partner = near_list[leaf_index, column]
            clamped = jnp.maximum(partner, 0)
            kernel_tile = matern(own_points, points[:, clamped])
            product = jnp.dot(by_leaf[:, clamped], kernel_tile.T, precision=HIGHEST)
            totals = totals + jnp.where(partner >= 0, product, 0.0)
        return totals
    near_part = lax.map(near_leaf, jnp.arange(leaves, dtype=jnp.int32))
    coefficients = jnp.einsum('pia,ira->irp', by_leaf, leaf_basis, precision=HIGHEST)
    skeletons = leaf_skeleton.reshape(3, leaves, RANK)

    def far_leaf(leaf_index):
        totals = jnp.zeros((RANK, PROBES), jnp.float32)
        for column in range(far_leaf_list.shape[1]):
            partner = far_leaf_list[leaf_index, column]
            clamped = jnp.maximum(partner, 0)
            kernel_tile = matern(skeletons[:, leaf_index], skeletons[:, clamped])
            product = jnp.dot(kernel_tile, coefficients[clamped], precision=HIGHEST)
            totals = totals + jnp.where(partner >= 0, product, 0.0)
        return totals
    leaf_far = lax.map(far_leaf, jnp.arange(leaves, dtype=jnp.int32))
    device_coef = jnp.einsum('irs,irp->isp', leaf_transfer, coefficients, precision=HIGHEST)
    device_coef = device_coef.reshape(devices, leaves // devices, RANK, PROBES).sum(axis=1)
    group_coef = jnp.einsum('qrs,qrp->qsp', device_transfer, device_coef, precision=HIGHEST)
    group_coef = group_coef.reshape(groups, devices // groups, RANK, PROBES).sum(axis=1)
    group_points = group_skeleton.reshape(3, groups, RANK)

    def far_group(group_index):
        totals = jnp.zeros((RANK, PROBES), jnp.float32)
        for column in range(far_group_list.shape[1]):
            partner = far_group_list[group_index, column]
            clamped = jnp.maximum(partner, 0)
            kernel_tile = matern(group_points[:, group_index], group_points[:, clamped])
            product = jnp.dot(kernel_tile, group_coef[clamped], precision=HIGHEST)
            totals = totals + jnp.where(partner >= 0, product, 0.0)
        return totals
    group_far = lax.map(far_group, jnp.arange(groups, dtype=jnp.int32))
    device_far = jnp.einsum('qrs,qsp->qrp', device_transfer, jnp.repeat(group_far, devices // groups, axis=0), precision=HIGHEST)
    leaf_total = leaf_far + jnp.einsum('irs,isp->irp', leaf_transfer, jnp.repeat(device_far, leaves // devices, axis=0), precision=HIGHEST)
    far_part = jnp.einsum('ira,irp->pia', leaf_basis, leaf_total, precision=HIGHEST)
    near_flat = jnp.transpose(near_part, (1, 0, 2)).reshape(PROBES, -1)
    return NOISE * vectors + near_flat + far_part.reshape(PROBES, -1)

def reference(probe_rhs, coords, near_list, far_leaf_list, far_group_list, leaf_basis, leaf_skeleton, leaf_transfer, device_transfer, group_skeleton):
    operator = partial(apply_operator, coords=coords, near_list=near_list, far_leaf_list=far_leaf_list, far_group_list=far_group_list, leaf_basis=leaf_basis, leaf_skeleton=leaf_skeleton, leaf_transfer=leaf_transfer, device_transfer=device_transfer, group_skeleton=group_skeleton)
    solution = jnp.zeros_like(probe_rhs)
    residual = probe_rhs
    direction = probe_rhs
    norm_now = lax.optimization_barrier(jnp.sum(residual * residual, axis=1))
    for iteration in range(ITERS):
        image_vec = operator(direction)
        step_length = norm_now / lax.optimization_barrier(jnp.sum(direction * image_vec, axis=1))
        solution = solution + step_length[:, None] * direction
        residual = residual - step_length[:, None] * image_vec
        if iteration + 1 < ITERS:
            norm_next = lax.optimization_barrier(jnp.sum(residual * residual, axis=1))
            direction = residual + (norm_next / norm_now)[:, None] * direction
            norm_now = norm_next
    return (solution, residual)
```

```python
import functools

import jax
import jax.numpy as jnp
from jax import lax
from jax.experimental import pallas as pl
from jax.experimental.pallas import tpu as pltpu
from jax.sharding import PartitionSpec as P

LEAF = 256
RANK = 64
PROBES = 32
REACH = 2
OWN = 4
Z = 16
C = 2
WIN = OWN + 2 * REACH
SPAN = (2 * REACH + 1) * LEAF
HALO = REACH * LEAF
POINTS = OWN * LEAF
HIGHEST = lax.Precision.HIGHEST
MESH = pl.DeviceIdType.MESH
F32 = jnp.float32
BF16 = jnp.bfloat16
ROWS = 32

(
    HALO_PTS,
    HALO_VEC,
    SKEL_Y,
    COEF_Y,
    GROUP_XC,
    GROUP_Z,
    TERM_PLANE,
    FAR_Z,
    SQUARE_Y,
    BASE_Y,
    FAR_Y,
    TERM_XC,
    FAR_Z2,
    HALO_VEC2,
    COEF_Y2,
    FAR_Y2,
    DOT_PLANE,
    DOT_Z,
    DOT_PLANE2,
    DOT_Z2,
    EXCHANGES,
) = range(21)


def dot_nn(a, b):
    return jnp.dot(a, b, precision=HIGHEST, preferred_element_type=F32)


def dot_nt(a, b):
    return lax.dot_general(
        a, b, (((1,), (1,)), ((), ())), precision=HIGHEST, preferred_element_type=F32
    )


def dot_16(a, b):
    return jnp.dot(a, b, preferred_element_type=F32)


def three(values):
    first = values.astype(BF16).astype(F32)
    rest = values - first
    second = rest.astype(BF16).astype(F32)
    return first, second, rest - second


def matern(square, weight):
    square = 5.0 * square
    scaled = square * lax.rsqrt(jnp.maximum(square, 1e-30))
    return (weight + weight * scaled + (weight * (1.0 / 3.0)) * square) * jnp.exp(-scaled)


def distances(columns, rows):
    total = None
    for axis in range(3):
        spread = columns[:, axis : axis + 1] - rows[axis : axis + 1, :]
        total = spread * spread if total is None else total + spread * spread
    return total


def put_tile(high, low, where, tile):
    first = tile.astype(BF16)
    high[where] = first
    low[where] = (tile - first.astype(F32)).astype(BF16)


def kernel(
    X,
    Y,
    near_list,
    far_list,
    rhs,
    coords,
    group_list,
    basis,
    leaf_skel,
    leaf_transfer,
    device_transfer,
    group_skel,
    sol,
    res,
    vwin,
    wwin,
    split,
    pts,
    pts_t,
    near_hi,
    near_lo,
    skel,
    skel_t,
    coef,
    coef2,
    csplit,
    leaf_hi,
    leaf_lo,
    pay,
    pay_xc,
    pay_z,
    tgt,
    gmask,
    group_hi,
    group_lo,
    ee,
    ee2,
    term,
    term_in,
    zout,
    zin,
    zout2,
    zin2,
    square,
    base,
    base_in,
    gf,
    gf2,
    gfull,
    gfull2,
    next_term,
    next_in,
    part,
    dots,
    dot_plane,
    dots_z,
    dot_z,
    dots2,
    dot_plane2,
    dots_z2,
    dot_z2,
    send,
    recv,
):
    chunk = PROBES // Y
    plane = X * Y * C
    targets = Z * RANK
    leaf_at = lax.axis_index("leaf")
    y = lax.axis_index("sub")
    c = lax.rem(leaf_at, C)
    z = lax.rem(leaf_at // C, Z)
    x = leaf_at // (C * Z)
    node = leaf_at * Y + y
    nodes = X * Z * C * Y
    place = (x * Y + y) * C + c

    def at_node(q):
        return {"leaf": q // Y, "sub": lax.rem(q, Y)}

    def at_plane(p):
        px = p // (Y * C)
        return {"leaf": (px * Z + z) * C + lax.rem(p, C), "sub": lax.rem(p // C, Y)}

    def at_xc(p):
        return {"leaf": ((p // C) * Z + z) * C + lax.rem(p, C), "sub": y}

    def at_y(p):
        return {"leaf": leaf_at, "sub": p}

    def at_z(p):
        return {"leaf": (x * Z + p) * C + c, "sub": y}

    after = lax.rem(node + 1, nodes)
    before = lax.rem(node + nodes - 1, nodes)

    def put(src, dst, stage, device):
        pltpu.make_async_remote_copy(
            src_ref=src,
            dst_ref=dst,
            send_sem=send.at[stage],
            recv_sem=recv.at[stage],
            device_id=device,
            device_id_type=MESH,
        ).start()

    def to_others(mine, count, step):
        def body(k, carry):
            step(lax.rem(mine + k, count))
            return carry

        lax.fori_loop(1, count, body, 0)

    def arrived(ref, stage):
        pltpu.make_async_copy(ref, ref, recv.at[stage]).wait()

    def left(ref, stage):
        pltpu.make_async_copy(ref, ref, send.at[stage]).wait()

    barrier = pltpu.get_barrier_semaphore()

    def signal(device):
        pl.semaphore_signal(barrier, inc=1, device_id=device, device_id_type=MESH)

    to_others(z, Z, lambda p: signal(at_z(p)))
    to_others(place, plane, lambda p: signal(at_plane(p)))
    signal(at_node(after))
    signal(at_node(before))

    lane128 = lax.broadcasted_iota(jnp.int32, (1, 2 * RANK), 1)

    pay[...] = jnp.zeros_like(pay)
    pay[0:3, 0:RANK] = group_skel[...]
    pay[0:3, RANK : 2 * RANK] = group_skel[...]
    pay[3:4, 0:16] = group_list[...].astype(F32)

    on_core = (lax.broadcasted_iota(jnp.int32, (2 * RANK, 1), 0) // RANK == c).astype(F32)
    for i in range(OWN):
        down = dot_nn(leaf_transfer[i], device_transfer[0])
        e = dot_nn(down.T, basis[i])
        cols = slice(i * LEAF, (i + 1) * LEAF)
        ee[:, cols] = e
        ee2[:, cols] = jnp.concatenate([e, e], axis=0) * on_core
    own = slice(HALO, HALO + POINTS)
    vwin[:, own] = rhs[...]
    term[...] = dot_nt(rhs[...], ee2[...]).reshape(Y, chunk, 2 * RANK)
    square[y] = dot_nt(ee[...], ee2[...])

    def coefficients(vec, out):
        for i in range(OWN):
            out[:, i * RANK : (i + 1) * RANK] = dot_nt(
                vec[:, HALO + i * LEAF : HALO + (i + 1) * LEAF], basis[i]
            )

    coefficients(vwin, part)
    coef[y] = part[...]

    pts[:, own] = jnp.zeros((8, POINTS), F32)
    pts[0:3, own] = coords[...]
    pts_t[HALO : HALO + POINTS, :] = pts[:, own].T
    skel[y] = jnp.zeros((8, OWN * RANK), F32)
    skel[y, 0:3, :] = leaf_skel[...]

    def near_tile(i, o):
        target = node * OWN + i + o - REACH
        weight = jnp.float32(0.0)
        for s in range(2 * REACH + 1):
            weight = weight + jnp.where(near_list[i, s] == target, 1.0, 0.0)
        weight = jnp.where(target >= 0, weight, 0.0)
        rows = pts[:, HALO + i * LEAF : HALO + (i + 1) * LEAF]

        def body(r, carry):
            columns = pts_t[pl.ds((i + o) * LEAF + r * ROWS, ROWS), :]
            tile = matern(distances(columns, rows), weight)
            put_tile(near_hi, near_lo, (i, pl.ds(o * LEAF + r * ROWS, ROWS), slice(None)), tile)
            return carry

        lax.fori_loop(0, LEAF // ROWS, body, 0)

    for i in range(OWN):
        for o in range(2 * REACH + 1):
            if REACH <= i + o < REACH + OWN:
                near_tile(i, o)

    pl.semaphore_wait(barrier, Z - 1 + plane - 1 + 2)

    to_others(
        place,
        plane,
        lambda p: put(
            term.at[lax.rem(p // C, Y)], term_in.at[place], TERM_PLANE, at_plane(p)
        ),
    )
    to_others(z, Z, lambda p: put(pay, pay_z.at[z], GROUP_Z, at_z(p)))
    to_others(x * C + c, X * C, lambda p: put(pay, pay_xc.at[x * C + c], GROUP_XC, at_xc(p)))
    low, high = slice(HALO, 2 * HALO), slice(POINTS, POINTS + HALO)
    to_low, to_high = slice(0, HALO), slice(HALO + POINTS, 2 * HALO + POINTS)
    put(pts.at[:, high], pts.at[:, to_low], HALO_PTS, at_node(after))
    put(pts.at[:, low], pts.at[:, to_high], HALO_PTS, at_node(before))
    to_others(y, Y, lambda p: put(skel.at[y], skel.at[y], SKEL_Y, at_y(p)))
    put(vwin.at[:, high], vwin.at[:, to_low], HALO_VEC, at_node(after))
    put(vwin.at[:, low], vwin.at[:, to_high], HALO_VEC, at_node(before))
    to_others(y, Y, lambda p: put(coef.at[y], coef.at[y], COEF_Y, at_y(p)))
    to_others(y, Y, lambda p: put(square.at[y], square.at[y], SQUARE_Y, at_y(p)))
    pay_z[z] = pay[...]
    pay_xc[x * C + c] = pay[...]
    term_in[place] = term[y]

    both = slice(0, 2 * HALO)
    arrived(pts.at[:, both], HALO_PTS)
    pts_t[0:HALO, :] = pts[:, to_low].T
    pts_t[HALO + POINTS : 2 * HALO + POINTS, :] = pts[:, to_high].T
    for i in range(OWN):
        for o in range(2 * REACH + 1):
            if not REACH <= i + o < REACH + OWN:
                near_tile(i, o)

    leaf_lane = lax.broadcasted_iota(jnp.int32, (1, OWN * RANK), 1) // RANK
    listed = []
    for s in range(8):
        row = jnp.full((1, OWN * RANK), -1, jnp.int32)
        for i in range(OWN):
            row = jnp.where(leaf_lane == i, far_list[i, s], row)
        listed.append(row)
    arrived(skel.at[pl.ds(0, Y - 1)], SKEL_Y)
    group_first = leaf_at * Y * OWN
    own_skel = skel[y]
    for d in range(Y):
        skel_t[d * OWN * RANK : (d + 1) * OWN * RANK, :] = skel[d].T

    def leaf_tile(m, carry):
        mask = jnp.zeros((1, OWN * RANK), F32)
        for row in listed:
            mask = mask + jnp.where(row == group_first + m, 1.0, 0.0)
        for r in range(RANK // ROWS):
            at = pl.ds(m * RANK + r * ROWS, ROWS)
            tile = matern(distances(skel_t[at, :], own_skel), mask)
            put_tile(leaf_hi, leaf_lo, (at, slice(None)), tile)
        return carry

    lax.fori_loop(0, Y * OWN, leaf_tile, 0)

    def three_of(vec):
        first, second, third = three(vec)
        split[0:PROBES, :] = first.astype(BF16)
        split[PROBES : 2 * PROBES, :] = second.astype(BF16)
        split[2 * PROBES : 3 * PROBES, :] = third.astype(BF16)

    def near_of(i):
        cols = slice(i * LEAF, i * LEAF + SPAN)
        a = dot_16(split[:, cols], near_hi[i])
        b = dot_16(split[0 : 2 * PROBES, cols], near_lo[i])
        return (
            (a[2 * PROBES :] + b[PROBES:])
            + (a[PROBES : 2 * PROBES] + b[0:PROBES])
            + a[0:PROBES]
        )

    def leaf_far(coefs):
        for d in range(Y):
            cols = slice(d * OWN * RANK, (d + 1) * OWN * RANK)
            first, second, third = three(coefs[d])
            csplit[0:PROBES, cols] = first.astype(BF16)
            csplit[PROBES : 2 * PROBES, cols] = second.astype(BF16)
            csplit[2 * PROBES : 3 * PROBES, cols] = third.astype(BF16)
        a = dot_16(csplit[...], leaf_hi[...])
        b = dot_16(csplit[0 : 2 * PROBES, :], leaf_lo[...])
        return (
            (a[2 * PROBES :] + b[PROBES:])
            + (a[PROBES : 2 * PROBES] + b[0:PROBES])
            + a[0:PROBES]
        )

    def local_image(vec, coefs, out):
        part[...] = leaf_far(coefs)
        for i in range(OWN):
            cols = slice(HALO + i * LEAF, HALO + (i + 1) * LEAF)
            far = dot_nn(part[:, i * RANK : (i + 1) * RANK], basis[i])
            out[:, cols] = vec[:, cols] + near_of(i) + far

    arrived(vwin.at[:, both], HALO_VEC)
    three_of(vwin[...])
    arrived(coef.at[pl.ds(0, Y - 1)], COEF_Y)
    local_image(vwin, coef, wwin)

    base[...] = dot_nt(wwin[:, own], ee2[...]).reshape(Y, chunk, 2 * RANK)
    to_others(y, Y, lambda p: put(base.at[p], base_in.at[y], BASE_Y, at_y(p)))
    base_in[y] = base[y]

    arrived(pay_xc.at[pl.ds(0, X * C - 1)], GROUP_XC)
    arrived(pay_z.at[pl.ds(0, Z - 1)], GROUP_Z)
    for k in range(Z // 2):
        tgt[:, k * 128 : (k + 1) * 128] = jnp.where(lane128 < RANK, pay_z[2 * k], pay_z[2 * k + 1])
    ids = lax.broadcasted_iota(jnp.int32, (1, targets), 1) // RANK
    ids = ((x * Z + ids) * C + c).astype(F32)

    def group_tile(h, carry):
        turned = pay_xc[h].T
        mask = jnp.sum(jnp.where(turned[0:16, 3:4] == ids, 1.0, 0.0), axis=0, keepdims=True)
        gmask[...] = mask
        for k in range(targets // 128):
            lanes = slice(k * 128, (k + 1) * 128)
            tile = matern(distances(turned[0:RANK, :], tgt[:, lanes]), gmask[:, lanes])
            put_tile(group_hi, group_lo, (pl.ds(h * RANK, RANK), lanes), tile)
        return carry

    lax.fori_loop(0, X * C, group_tile, 0)

    def group_far(sources, out):
        terms = [three(s) for s in sources]
        stacked = [jnp.concatenate([t[k] for t in terms], axis=1) for k in range(3)]
        stacked.append(jnp.zeros_like(stacked[0]))
        stacked = jnp.concatenate(stacked, axis=0).astype(BF16)
        a = dot_16(stacked, group_hi[...])
        b = dot_16(stacked, group_lo[...])
        a = [a[k * chunk : (k + 1) * chunk] for k in range(3)]
        b = [b[k * chunk : (k + 1) * chunk] for k in range(2)]
        total = (a[2] + b[1]) + (a[1] + b[0]) + a[0]
        for k in range(Z):
            out[k] = total[:, k * RANK : (k + 1) * RANK]

    def summed(ref, count, first=0):
        total = ref[first]
        for k in range(1, count):
            total = total + ref[first + k]
        return total

    arrived(term_in.at[pl.ds(0, plane - 1)], TERM_PLANE)
    group_far([summed(term_in, Y * C, k * Y * C) for k in range(X)], zout)
    to_others(z, Z, lambda p: put(zout.at[p], zin.at[z], FAR_Z, at_z(p)))
    zin[z] = zout[z]
    first_term = summed(term_in, Y * C, x * Y * C) * (lane128 // RANK == c).astype(F32)

    arrived(base_in.at[pl.ds(0, Y - 1)], BASE_Y)
    base_sum = summed(base_in, Y)
    arrived(square.at[pl.ds(0, Y - 1)], SQUARE_Y)
    square_sum = summed(square, Y)

    row_of = lax.broadcasted_iota(jnp.int32, (PROBES, 1), 0)
    own_rows = (row_of // chunk == y).astype(F32)

    def lanes_of(a, b, width=POINTS):
        total = a[:, 0:128] * b[:, 0:128]
        for k in range(1, width // 128):
            cols = slice(k * 128, (k + 1) * 128)
            total = total + a[:, cols] * b[:, cols]
        return total

    ones = jnp.ones((8, 128), F32)

    def total_lanes(parts):
        parts = parts + [jnp.zeros((PROBES, 128), F32)] * (4 - len(parts))
        return dot_nt(ones, jnp.concatenate(parts, axis=0))[0:1, :]

    def all_rows(block):
        return jnp.concatenate([block] * Y, axis=0)

    rhs_now = rhs[...]
    rr_lanes = lanes_of(rhs_now, rhs_now)
    curve_lanes = lanes_of(rhs_now, wwin[:, own])

    arrived(zin.at[pl.ds(0, Z - 1)], FAR_Z)
    got = summed(zin, Z)
    gf[...] = got
    following = base_sum + dot_nn(got, square_sum)
    next_term[...] = following
    to_others(
        x * C + c, X * C, lambda p: put(next_term, next_in.at[x * C + c], TERM_XC, at_xc(p))
    )
    to_others(y, Y, lambda p: put(gf, gfull.at[y], FAR_Y, at_y(p)))
    next_in[x * C + c] = following
    gfull[y] = got
    twice = jnp.concatenate([got, got], axis=1)
    dots[...] = total_lanes([rr_lanes, curve_lanes + own_rows * all_rows(first_term * twice)])
    to_others(place, plane, lambda p: put(dots, dot_plane.at[place], DOT_PLANE, at_plane(p)))
    dot_plane[place] = dots[...]

    arrived(gfull.at[pl.ds(0, Y - 1)], FAR_Y)
    wwin[:, own] = wwin[:, own] + dot_nn(gfull[...].reshape(PROBES, RANK), ee[...])
    put(wwin.at[:, high], wwin.at[:, to_low], HALO_VEC2, at_node(after))
    put(wwin.at[:, low], wwin.at[:, to_high], HALO_VEC2, at_node(before))
    coefficients(wwin, part)
    coef2[y] = part[...]
    to_others(y, Y, lambda p: put(coef2.at[y], coef2.at[y], COEF_Y2, at_y(p)))

    arrived(next_in.at[pl.ds(0, X * C - 1)], TERM_XC)
    group_far([summed(next_in, C, k * C) for k in range(X)], zout2)
    to_others(z, Z, lambda p: put(zout2.at[p], zin2.at[z], FAR_Z2, at_z(p)))
    zin2[z] = zout2[z]

    arrived(dot_plane.at[pl.ds(0, plane - 1)], DOT_PLANE)
    plane_sum = jnp.sum(dot_plane[...], axis=0)
    dots_z[...] = plane_sum
    to_others(z, Z, lambda p: put(dots_z, dot_z.at[z], DOT_Z, at_z(p)))
    dot_z[z] = plane_sum

    arrived(wwin.at[:, both], HALO_VEC2)
    three_of(wwin[...])
    arrived(coef2.at[pl.ds(0, Y - 1)], COEF_Y2)
    left(vwin.at[:, both], HALO_VEC)
    local_image(wwin, coef2, vwin)

    lane_of = lax.broadcasted_iota(jnp.int32, (PROBES, 128), 1)

    def column(row, k):
        hit = (lane_of == row_of + k * PROBES).astype(F32)
        return jnp.sum(hit * row, axis=1, keepdims=True)

    arrived(zin2.at[pl.ds(0, Z - 1)], FAR_Z2)
    got2 = summed(zin2, Z)
    gf2[...] = got2
    to_others(y, Y, lambda p: put(gf2, gfull2.at[y], FAR_Y2, at_y(p)))
    gfull2[y] = got2
    twice2 = jnp.concatenate([got2, got2], axis=1)
    first_far = own_rows * all_rows(first_term * twice2)
    second_far = own_rows * all_rows(following * twice2)

    arrived(dot_z.at[pl.ds(0, Z - 1)], DOT_Z)
    sums = jnp.sum(dot_z[...], axis=0)
    rr0 = column(sums, 0)
    curve0 = column(sums, 1)
    step0 = rr0 / curve0
    image1 = wwin[:, own]
    image2 = vwin[:, own]
    residual1 = rhs_now - step0 * image1
    turned_lanes = lanes_of(residual1, image1)
    dots2[...] = total_lanes(
        [
            lanes_of(residual1, residual1),
            turned_lanes - step0 * (lanes_of(residual1, image2) + first_far - step0 * second_far),
            turned_lanes - step0 * (lanes_of(rhs_now, image2) + first_far),
        ]
    )
    to_others(place, plane, lambda p: put(dots2, dot_plane2.at[place], DOT_PLANE2, at_plane(p)))
    dot_plane2[place] = dots2[...]

    arrived(gfull2.at[pl.ds(0, Y - 1)], FAR_Y2)
    image2 = image2 + dot_nn(gfull2[...].reshape(PROBES, RANK), ee[...])
    turned1 = image1 - step0 * image2

    arrived(dot_plane2.at[pl.ds(0, plane - 1)], DOT_PLANE2)
    plane_sum2 = jnp.sum(dot_plane2[...], axis=0)
    dots_z2[...] = plane_sum2
    to_others(z, Z, lambda p: put(dots_z2, dot_z2.at[z], DOT_Z2, at_z(p)))
    dot_z2[z] = plane_sum2
    arrived(dot_z2.at[pl.ds(0, Z - 1)], DOT_Z2)
    sums2 = jnp.sum(dot_z2[...], axis=0)
    rr1 = column(sums2, 0)
    ratio = rr1 / rr0
    curve1 = column(sums2, 1) + ratio * (column(sums2, 2) + curve0) + ratio * ratio * curve0
    step1 = rr1 / curve1
    direction1 = residual1 + ratio * rhs_now
    sol[...] = step0 * rhs_now + step1 * direction1
    res[...] = residual1 - step1 * (turned1 + ratio * image1)

    left(pts.at[:, both], HALO_PTS)
    left(wwin.at[:, both], HALO_VEC2)
    for ref, stage in (
        (skel, SKEL_Y),
        (coef, COEF_Y),
        (coef2, COEF_Y2),
        (square, SQUARE_Y),
        (base_in, BASE_Y),
        (gfull, FAR_Y),
        (gfull2, FAR_Y2),
    ):
        left(ref.at[pl.ds(0, Y - 1)], stage)
    for ref, stage in ((pay_z, GROUP_Z), (zin, FAR_Z), (zin2, FAR_Z2), (dot_z, DOT_Z), (dot_z2, DOT_Z2)):
        left(ref.at[pl.ds(0, Z - 1)], stage)
    left(pay_xc.at[pl.ds(0, X * C - 1)], GROUP_XC)
    left(term_in.at[pl.ds(0, plane - 1)], TERM_PLANE)
    left(next_in.at[pl.ds(0, X * C - 1)], TERM_XC)
    left(dot_plane.at[pl.ds(0, plane - 1)], DOT_PLANE)
    left(dot_plane2.at[pl.ds(0, plane - 1)], DOT_PLANE2)


def shards(X, Y, rhs, coords, near_list, far_list, group_list, basis, skel, transfer, device, group):
    chunk = PROBES // Y
    plane = X * Y * C
    targets = Z * RANK
    sources = X * C * RANK
    window = WIN * LEAF
    own_rank = OWN * RANK

    def f32(*shape):
        return pltpu.VMEM(shape, F32)

    def b16(*shape):
        return pltpu.VMEM(shape, BF16)

    vmem = pl.BlockSpec(memory_space=pltpu.VMEM)
    smem = pl.BlockSpec(memory_space=pltpu.SMEM)
    block = jax.ShapeDtypeStruct((PROBES, POINTS), F32)
    return pl.pallas_call(
        functools.partial(kernel, X, Y),
        out_shape=(block, block),
        in_specs=[smem, smem] + [vmem] * 8,
        out_specs=(vmem, vmem),
        scratch_shapes=[
            f32(PROBES, window),
            f32(PROBES, window),
            b16(3 * PROBES, window),
            f32(8, window),
            f32(window, 8),
            b16(OWN, SPAN, LEAF),
            b16(OWN, SPAN, LEAF),
            f32(Y, 8, own_rank),
            f32(Y * own_rank, 8),
            f32(Y, PROBES, own_rank),
            f32(Y, PROBES, own_rank),
            b16(3 * PROBES, Y * own_rank),
            b16(Y * own_rank, own_rank),
            b16(Y * own_rank, own_rank),
            f32(8, 128),
            f32(X * C, 8, 128),
            f32(Z, 8, 128),
            f32(8, targets),
            f32(1, targets),
            b16(sources, targets),
            b16(sources, targets),
            f32(RANK, POINTS),
            f32(2 * RANK, POINTS),
            f32(Y, chunk, 2 * RANK),
            f32(plane, chunk, 2 * RANK),
            f32(Z, chunk, RANK),
            f32(Z, chunk, RANK),
            f32(Z, chunk, RANK),
            f32(Z, chunk, RANK),
            f32(Y, RANK, 2 * RANK),
            f32(Y, chunk, 2 * RANK),
            f32(Y, chunk, 2 * RANK),
            f32(chunk, RANK),
            f32(chunk, RANK),
            f32(Y, chunk, RANK),
            f32(Y, chunk, RANK),
            f32(chunk, 2 * RANK),
            f32(X * C, chunk, 2 * RANK),
            f32(PROBES, own_rank),
            f32(1, 128),
            f32(plane, 1, 128),
            f32(1, 128),
            f32(Z, 1, 128),
            f32(1, 128),
            f32(plane, 1, 128),
            f32(1, 128),
            f32(Z, 1, 128),
            pltpu.SemaphoreType.DMA((EXCHANGES,)),
            pltpu.SemaphoreType.DMA((EXCHANGES,)),
        ],
        compiler_params=pltpu.CompilerParams(
            collective_id=0, has_side_effects=True, vmem_limit_bytes=40 * 2**20
        ),
    )(near_list, far_list, rhs, coords, group_list, basis, skel, transfer, device, group)


def solution(mesh):
    both = ("leaf", "sub")
    X, Y = mesh.shape["leaf"] // (Z * C), mesh.shape["sub"]
    in_specs = (
        P(None, both),
        P(None, both),
        P(both, None),
        P(both, None),
        P("leaf", None),
        P(both, None, None),
        P(None, both),
        P(both, None, None),
        P(both, None, None),
        P(None, "leaf"),
    )
    out_specs = (P(None, both), P(None, both))
    return jax.shard_map(
        functools.partial(shards, X, Y),
        mesh=mesh,
        in_specs=in_specs,
        out_specs=out_specs,
        check_vma=False,
    )
```
